32 devices in a mesh: row: 8 (over z, y), col: 4 (over x, core).
Axes of the slice: x: 2, y: 2, z: 4, core: 2. Of those that a mesh axis runs over, the one named last changes fastest.
Arguments:
- acts: bfloat16 [16384, 4096], P('row', 'col'), may hold values from -6 to 6
- out_grads: bfloat16 [16384, 1, 4096], P('row', None, 'col'), may hold values from -0.0234375 to 0.0234375
- row_stat: float32 [1, 4096], P(None, 'row'), may hold values from 0.02 to 0.2
- col_stat: float32 [1, 4096], P(None, 'col'), may hold values from 0.02 to 0.2
- master: float32 [4096, 1, 4096], P('row', None, 'col'), may hold values from -0.09375 to 0.09375
Outputs:
- fresh_weights: bfloat16 [4096, 1, 4096], P(None, None, 'col')
- master_out: float32 [4096, 1, 4096], P('row', None, 'col')
- update_out: float32 [4096, 1, 4096], P('row', None, 'col')
- row_out: float32 [1, 4096], P(None, 'row')
- col_out: float32 [1, 4096], P(None, 'col')
The draws below stay inside these ranges and needn't reach their ends.
All inputs are finite; a program needn't handle non-finite values.
Results may differ from the reference program's by a relative error of at most 0.001.
Values may be sent and summed in bfloat16 or wider, within the bound.
A program may use at most 256 MiB of HBM per device.

```python
import math
import jax
import jax.numpy as jnp
from jax import lax

D = 4096
MATS = 1
TOKENS = 16384


def strengthened(drawn, stream_key, source, target, blocks, factor):
    owner, partner = [(jnp.arange(drawn.shape[dim]) // (drawn.shape[dim] // blocks)).reshape([-1 if axis == dim else 1 for axis in range(drawn.ndim)]) for dim in (source, target)]
    chosen = jax.random.permutation(stream_key, blocks)[partner]
    strong = (owner == chosen) | (owner == (partner + blocks // 2) % blocks)
    return jnp.where(strong, factor * drawn, drawn)


def levels(own_key, extent, cuts, low, high):
    def one(dim, blocks):
        steps = jax.random.uniform(jax.random.fold_in(jax.random.fold_in(own_key, 6), dim), (blocks,), jnp.float32, low / len(cuts), high / len(cuts))
        return jnp.repeat(jnp.exp(steps), extent[dim] // blocks).reshape((-1,) + (1,) * (len(extent) - dim - 1))

    level = one(*cuts[0])
    for cut in cuts[1:]:
        level = level * one(*cut)
    return level


def normal_values(own_key, dims, scale, bound, cuts=(), dtype=jnp.bfloat16):
    drawn = scale * jax.random.normal(own_key, dims, jnp.float32)
    if cuts:
        drawn = drawn * levels(own_key, dims, cuts, -0.22, 0.18)
    return jnp.clip(drawn, -bound, bound).astype(dtype)


def noise_with(stream_key, shape, spread, reach, cuts, heavy, kind=jnp.bfloat16):
    result = spread * jax.random.normal(stream_key, shape, jnp.float32)
    if cuts:
        result = result * levels(stream_key, shape, cuts, -0.22, 0.18)
    return jnp.clip(strengthened(result, jax.random.fold_in(stream_key, 3), *heavy), -reach, reach).astype(kind)


def setup_inputs(seed: int = 0) -> dict:
    key_list = jax.random.split(jax.random.key(seed), 6)
    return {
        "acts": noise_with(key_list[0], (TOKENS, D), 1.0, 6.0, ((0, 8), (1, 4)), (0, 1, 8, 2.0)),
        "out_grads": normal_values(key_list[1], (TOKENS, MATS, D), (0.5 / TOKENS ** 0.5), 0.0234375, ((0, 8), (2, 4))),
        "row_stat": jnp.clip(jnp.exp(math.log(0.2) - 2.3025851 * jax.random.uniform(key_list[2], (MATS, D), jnp.float32) ** levels(key_list[2], (MATS, D), ((1, 8),), -0.2, 0.2)), 0.02, 0.2),
        "col_stat": jnp.clip(jnp.exp(math.log(0.2) - 2.3025851 * jax.random.uniform(key_list[3], (MATS, D), jnp.float32) ** levels(key_list[3], (MATS, D), ((1, 4),), -0.2, 0.2)), 0.02, 0.2),
        "master": normal_values(key_list[4], (D, MATS, D), D ** -0.5, 0.09375, ((0, 8), (2, 4)), jnp.float32),
    }


def reference(acts, out_grads, row_stat, col_stat, master):
    flat = out_grads.reshape(TOKENS, MATS * D)
    grad = jnp.dot(acts.T, flat, preferred_element_type=jnp.float32).reshape(D, MATS, D)
    squares = grad * grad + 1e-30
    row_out = 0.75 * row_stat + 0.25 * lax.optimization_barrier(jnp.sum(squares, axis=2)).T / D
    col_out = 0.75 * col_stat + 0.25 * lax.optimization_barrier(jnp.sum(squares, axis=0)) / D
    row_mean = lax.optimization_barrier(jnp.sum(row_out, axis=1)) / D
    raw = grad * lax.rsqrt(row_out.T[:, :, None] * col_out[None, :, :] / row_mean[None, :, None])
    rms = jnp.sqrt(lax.optimization_barrier(jnp.sum(raw * raw, axis=(0, 2))) / (D * D))
    update_out = raw / jnp.maximum(1.0, rms)[None, :, None]
    master_out = master - 0.01 * update_out
    return (master_out.astype(jnp.bfloat16), master_out, update_out, row_out, col_out)
```

```python
import jax
import jax.numpy as jnp
from jax import lax
from jax.sharding import PartitionSpec as P

D = 4096


def contract_tokens(left, right):
    return lax.dot_general(
        left, right, (((0,), (0,)), ((), ())), preferred_element_type=jnp.float32
    )


def pair_sum(part, axis, partner_bit, mine, scale):
    n = lax.axis_size("row")
    keep = lax.dynamic_index_in_dim(part, mine, axis, keepdims=False)
    give = lax.dynamic_index_in_dim(part, 1 - mine, axis, keepdims=False)
    got = lax.ppermute(
        (give * scale).astype(jnp.float16), "row", [(r, r ^ partner_bit) for r in range(n)]
    )
    return keep + got.astype(jnp.float32) / scale


def reduce_blocks(part, r, y_first, scale):
    y, z_lo, z_hi = r % 2, (r // 2) % 2, r // 4
    if y_first:
        part = pair_sum(part, 2, 1, y, scale)
        part = pair_sum(part, 1, 2, z_lo, scale)
        return pair_sum(part, 0, 4, z_hi, scale)
    part = pair_sum(part, 1, 2, z_lo, scale)
    part = pair_sum(part, 0, 4, z_hi, scale)
    return pair_sum(part, 0, 1, y, scale)


def gradient_rows(acts, flat_out):
    tok, width = acts.shape
    cols = flat_out.shape[1]
    r = lax.axis_index("row")
    top = lax.pmax(jnp.max(jnp.abs(flat_out)).astype(jnp.float32), "row")
    scale = 16384.0 / (6.0 * tok * lax.axis_size("row") * jnp.maximum(top, 1e-30))
    step = width // 4
    pieces = []
    for k in range(2):
        mine = acts.reshape(tok, 2, 2, step)[:, :, k].reshape(tok, 2 * step)
        full = lax.all_gather(mine, "col", axis=1, tiled=True)
        half = cols // 2
        sums = []
        for j in range(2):
            part = contract_tokens(full, flat_out[:, j * half : (j + 1) * half])
            part = part.reshape(2, 2, 2, step, half)
            sums.append(reduce_blocks(part, r, j == 0, scale))
        pieces.append(jnp.concatenate(sums, axis=1))
    return jnp.concatenate(pieces, axis=0)


def shards(acts, out_grads, row_stat, col_stat, master):
    tok_here, mats, width_c = out_grads.shape
    flat_out = out_grads.reshape(tok_here, mats * width_c)
    rows_here = master.shape[0]
    if (lax.axis_size("row"), lax.axis_size("col")) == (8, 4):
        grad = gradient_rows(acts, flat_out)
    else:
        acts_full = lax.all_gather(acts, "col", axis=1, tiled=True)
        grad = lax.psum_scatter(
            contract_tokens(acts_full, flat_out), "row", scatter_dimension=0, tiled=True
        )
    grad = grad.reshape(rows_here, mats, width_c)
    squares = grad * grad + 1e-30
    row_part = jnp.sum(squares, axis=2).T
    col_part = jnp.sum(squares, axis=0)
    row_sum = lax.psum(row_part, "col")
    row_out = 0.75 * row_stat + 0.25 * row_sum / D
    col_sum, row_total = lax.psum((col_part, jnp.sum(row_out, axis=1)), "row")
    col_out = 0.75 * col_stat + 0.25 * col_sum / D
    row_mean = row_total / D
    raw = grad * lax.rsqrt(row_out.T[:, :, None] * col_out[None, :, :] / row_mean[None, :, None])
    total_sq = lax.psum(jnp.sum(raw * raw, axis=(0, 2)), ("row", "col"))
    rms = jnp.sqrt(total_sq / (D * D))
    update_out = raw / jnp.maximum(1.0, rms)[None, :, None]
    master_out = master - 0.01 * update_out
    fresh = lax.all_gather(master_out.astype(jnp.bfloat16), "row", axis=0, tiled=True)
    return (fresh, master_out, update_out, row_out, col_out)


def solution(mesh):
    in_specs = (
        P("row", "col"),
        P("row", None, "col"),
        P(None, "row"),
        P(None, "col"),
        P("row", None, "col"),
    )
    out_specs = (
        P(None, None, "col"),
        P("row", None, "col"),
        P("row", None, "col"),
        P(None, "row"),
        P(None, "col"),
    )
    return jax.shard_map(shards, mesh=mesh, in_specs=in_specs, out_specs=out_specs, check_vma=False)
```

```python
import functools

import jax
import jax.numpy as jnp
from jax import lax
from jax.experimental import pallas as pl
from jax.experimental.pallas import tpu as pltpu
from jax.sharding import PartitionSpec as P

D = 4096


def contract_tokens(left, right):
    return lax.dot_general(
        left, right, (((0,), (0,)), ((), ())), preferred_element_type=jnp.float32
    )


def pair_sum(part, axis, partner_bit, mine, scale):
    n = lax.axis_size("row")
    keep = lax.dynamic_index_in_dim(part, mine, axis, keepdims=False)
    give = lax.dynamic_index_in_dim(part, 1 - mine, axis, keepdims=False)
    got = lax.ppermute(
        (give * scale).astype(jnp.float16), "row", [(r, r ^ partner_bit) for r in range(n)]
    )
    return keep + got.astype(jnp.float32) / scale


def reduce_blocks(part, r, y_first, scale):
    y, z_lo, z_hi = r % 2, (r // 2) % 2, r // 4
    if y_first:
        part = pair_sum(part, 2, 1, y, scale)
        part = pair_sum(part, 1, 2, z_lo, scale)
        return pair_sum(part, 0, 4, z_hi, scale)
    part = pair_sum(part, 1, 2, z_lo, scale)
    part = pair_sum(part, 0, 4, z_hi, scale)
    return pair_sum(part, 0, 1, y, scale)


def gradient_rows(acts, flat_out):
    tok, width = acts.shape
    cols = flat_out.shape[1]
    r = lax.axis_index("row")
    top = lax.pmax(jnp.max(jnp.abs(flat_out)).astype(jnp.float32), "row")
    scale = 16384.0 / (6.0 * tok * lax.axis_size("row") * jnp.maximum(top, 1e-30))
    step = width // 4
    pieces = []
    for k in range(2):
        mine = acts.reshape(tok, 2, 2, step)[:, :, k].reshape(tok, 2 * step)
        full = lax.all_gather(mine, "col", axis=1, tiled=True)
        half = cols // 2
        sums = []
        for j in range(2):
            part = contract_tokens(full, flat_out[:, j * half : (j + 1) * half])
            part = part.reshape(2, 2, 2, step, half)
            sums.append(reduce_blocks(part, r, j == 0, scale))
        pieces.append(jnp.concatenate(sums, axis=1))
    return jnp.concatenate(pieces, axis=0)


MESH = pl.DeviceIdType.MESH
CHUNK = 64


def exchange(axis, n, source, slots, send, recv):
    me = lax.axis_index(axis)

    def copy(to, slot):
        return pltpu.make_async_remote_copy(
            src_ref=source,
            dst_ref=slots.at[slot],
            send_sem=send.at[to],
            recv_sem=recv.at[slot],
            device_id={axis: to},
            device_id_type=MESH,
        )

    def start():
        for k in range(1, n):
            copy(lax.rem(me + k, n), me).start()
        slots[me] = source[...]

    def finish():
        for k in range(1, n):
            peer = lax.rem(me + k, n)
            copy(peer, peer).wait_recv()
        for k in range(1, n):
            copy(lax.rem(me + k, n), me).wait_send()

    return start, finish


def tail_kernel(
    rows_n, cols_n, grad, row_part, col_part, row_stat, col_stat, master,
    fresh, master_out, update, row_out, col_out,
    row_slots, col_slots, row_tall, pair, pair_slots, one, one_slots,
    rs, rr, cs, cr, ps, pr, os, orr, item_send, item_recv,
):
    r, c = lax.axis_index("row"), lax.axis_index("col")
    height, width = grad.shape
    y, z = lax.rem(r, 2), r // 2
    depth = rows_n // 2
    barrier = pltpu.get_barrier_semaphore()
    for k in range(1, rows_n):
        pl.semaphore_signal(barrier, inc=1, device_id={"row": lax.rem(r + k, rows_n)}, device_id_type=MESH)
    for k in range(1, cols_n):
        pl.semaphore_signal(barrier, inc=1, device_id={"col": lax.rem(c + k, cols_n)}, device_id_type=MESH)
    pl.semaphore_wait(barrier, rows_n + cols_n - 2)

    start_c, finish_c = exchange("row", rows_n, col_part, col_slots, cs, cr)
    start_r, finish_r = exchange("col", cols_n, row_part, row_slots, rs, rr)
    start_c()
    start_r()
    finish_r()
    new_row = 0.75 * row_stat[...] + 0.25 * jnp.sum(row_slots[...], axis=0) / D
    row_out[...] = new_row[0:1]
    row_tall[...] = jnp.transpose(jnp.broadcast_to(new_row[0:1], (128, height)))
    pair[8:16] = jnp.broadcast_to(jnp.sum(new_row, axis=1, keepdims=True), (8, 128))
    finish_c()
    new_col = 0.75 * col_stat[...] + 0.25 * jnp.sum(col_slots[...], axis=0) / D
    col_out[...] = new_col[0:1]

    def scaled(i, total):
        here = pl.ds(pl.multiple_of(i * CHUNK, CHUNK), CHUNK)
        value = grad[here] * lax.rsqrt(row_tall[here][:, 0:1] * col_out[...])
        update[here] = value
        return total + jnp.sum((value * value).reshape(CHUNK // 8, 8, width), axis=0)

    total = lax.fori_loop(0, height // CHUNK, scaled, jnp.zeros((8, width), jnp.float32))
    total = jnp.sum(jnp.sum(total, axis=0, keepdims=True), axis=1, keepdims=True)
    pair[0:8] = jnp.broadcast_to(total, (8, 128))
    start_p, finish_p = exchange("row", rows_n, pair, pair_slots, ps, pr)
    start_p()
    finish_p()
    both = jnp.sum(pair_slots[...], axis=0)
    one[...] = both[0:8]
    start_o, finish_o = exchange("col", cols_n, one, one_slots, os, orr)
    start_o()
    finish_o()
    mean = both[8:16] / D
    rms = jnp.sqrt(jnp.sum(one_slots[...], axis=0) * mean / (D * D))
    factor = (jnp.sqrt(mean) / jnp.maximum(1.0, rms))[0:1, 0:1]

    def finished(i, carry):
        here = pl.ds(pl.multiple_of(i * CHUNK, CHUNK), CHUNK)
        value = update[here] * factor
        update[here] = value
        value = master[here] - 0.01 * value
        master_out[here] = value
        fresh[pl.ds(pl.multiple_of(r * height + i * CHUNK, CHUNK), CHUNK)] = value.astype(jnp.bfloat16)
        return carry

    piece = height // 2

    def item(zs, ys, half, way):
        number = (zs * 2 + ys) * 2 + half
        place = fresh.at[pl.ds(pl.multiple_of(number * piece, piece), piece)]
        target = r + (1 - 2 * y) if way == 0 else (r + 2 if way == 1 else r - 2)
        return pltpu.make_async_remote_copy(
            src_ref=place,
            dst_ref=place,
            send_sem=item_send.at[number * 3 + way],
            recv_sem=item_recv.at[number],
            device_id={"row": target},
            device_id_type=MESH,
        )

    def along(zs, ys, half, way, act):
        @pl.when(z < depth - 1 if way == 1 else z > 0)
        def _():
            act(item(zs, ys, half, way))

    def begin(copy):
        copy.start()

    def sent(copy):
        copy.wait_send()

    def arrived(copy):
        copy.wait_recv()

    lax.fori_loop(0, height // CHUNK // 2, finished, 0)
    item(z, y, 0, 0).start()
    for way in (1, 2):
        along(z, y, 0, way, begin)
    lax.fori_loop(height // CHUNK // 2, height // CHUNK, finished, 0)
    for way in (1, 2):
        along(z, y, 1, way, begin)
    item(z, y, 1, 0).start()
    item(z, 1 - y, 0, 0).wait_recv()
    for way in (1, 2):
        along(z, 1 - y, 0, way, begin)

    kinds = ((y, 0), (y, 1), (1 - y, 0))

    def each(k, way, do):
        zs = z - k if way == 1 else z + k

        @pl.when(zs >= 0 if way == 1 else zs < depth)
        def _():
            do(zs)

    for k in range(1, depth):
        for ys, half in kinds:
            for way in (1, 2):
                def pass_on(zs, ys=ys, half=half, way=way):
                    arrived(item(zs, ys, half, 0))
                    along(zs, ys, half, way, begin)
                    if half == 1:
                        item(zs, ys, half, 0).start()

                each(k, way, pass_on)

    for k in range(depth):
        for way in (1, 2) if k else (1,):
            def last(zs):
                arrived(item(zs, 1 - y, 1, 0))
                sent(item(zs, y, 1, 0))

            each(k, way, last)
    item(z, y, 0, 0).wait_send()
    for k in range(depth):
        for ys, half in kinds:
            for way in (1, 2):
                def drain(zs, ys=ys, half=half, way=way):
                    along(zs, ys, half, way, sent)

                each(k, way, drain)


def tail(grad, row_part, col_part, row_stat, col_stat, master):
    rows_n, cols_n = lax.axis_size("row"), lax.axis_size("col")
    height, width = grad.shape
    f32 = jnp.float32

    def eight(x):
        return jnp.broadcast_to(x, (8, x.shape[1]))

    vmem = pl.BlockSpec(memory_space=pltpu.VMEM)
    dma = pltpu.SemaphoreType.DMA
    items = rows_n * 2
    return pl.pallas_call(
        functools.partial(tail_kernel, rows_n, cols_n),
        out_shape=(
            jax.ShapeDtypeStruct((rows_n * height, width), jnp.bfloat16),
            jax.ShapeDtypeStruct((height, width), f32),
            jax.ShapeDtypeStruct((height, width), f32),
            jax.ShapeDtypeStruct((1, height), f32),
            jax.ShapeDtypeStruct((1, width), f32),
        ),
        in_specs=[vmem] * 6,
        out_specs=(vmem,) * 5,
        scratch_shapes=[
            pltpu.VMEM((cols_n, 8, height), f32),
            pltpu.VMEM((rows_n, 8, width), f32),
            pltpu.VMEM((height, 128), f32),
            pltpu.VMEM((16, 128), f32),
            pltpu.VMEM((rows_n, 16, 128), f32),
            pltpu.VMEM((8, 128), f32),
            pltpu.VMEM((cols_n, 8, 128), f32),
            dma((cols_n,)), dma((cols_n,)),
            dma((rows_n,)), dma((rows_n,)),
            dma((rows_n,)), dma((rows_n,)),
            dma((cols_n,)), dma((cols_n,)),
            dma((items * 3,)), dma((items,)),
        ],
        compiler_params=pltpu.CompilerParams(
            collective_id=0, has_side_effects=True, vmem_limit_bytes=40 * 1024 * 1024
        ),
    )(grad, eight(row_part), eight(col_part), eight(row_stat), eight(col_stat), master)


def shards(acts, out_grads, row_stat, col_stat, master):
    tok_here, mats, width_c = out_grads.shape
    flat_out = out_grads.reshape(tok_here, mats * width_c)
    rows_here = master.shape[0]
    if (lax.axis_size("row"), lax.axis_size("col"), mats) == (8, 4, 1):
        grad = gradient_rows(acts, flat_out)
        squares = grad * grad + 1e-30
        fresh, master_out, update_out, row_out, col_out = tail(
            grad,
            jnp.sum(squares, axis=1)[None],
            jnp.sum(squares, axis=0)[None],
            row_stat,
            col_stat,
            master.reshape(rows_here, width_c),
        )
        return (
            fresh.reshape(-1, mats, width_c),
            master_out.reshape(master.shape),
            update_out.reshape(master.shape),
            row_out,
            col_out,
        )
    else:
        acts_full = lax.all_gather(acts, "col", axis=1, tiled=True)
        grad = lax.psum_scatter(
            contract_tokens(acts_full, flat_out), "row", scatter_dimension=0, tiled=True
        )
    grad = grad.reshape(rows_here, mats, width_c)
    squares = grad * grad + 1e-30
    row_part = jnp.sum(squares, axis=2).T
    col_part = jnp.sum(squares, axis=0)
    row_sum = lax.psum(row_part, "col")
    row_out = 0.75 * row_stat + 0.25 * row_sum / D
    col_sum, row_total = lax.psum((col_part, jnp.sum(row_out, axis=1)), "row")
    col_out = 0.75 * col_stat + 0.25 * col_sum / D
    row_mean = row_total / D
    raw = grad * lax.rsqrt(row_out.T[:, :, None] * col_out[None, :, :] / row_mean[None, :, None])
    total_sq = lax.psum(jnp.sum(raw * raw, axis=(0, 2)), ("row", "col"))
    rms = jnp.sqrt(total_sq / (D * D))
    update_out = raw / jnp.maximum(1.0, rms)[None, :, None]
    master_out = master - 0.01 * update_out
    fresh = lax.all_gather(master_out.astype(jnp.bfloat16), "row", axis=0, tiled=True)
    return (fresh, master_out, update_out, row_out, col_out)


def solution(mesh):
    in_specs = (
        P("row", "col"),
        P("row", None, "col"),
        P(None, "row"),
        P(None, "col"),
        P("row", None, "col"),
    )
    out_specs = (
        P(None, None, "col"),
        P("row", None, "col"),
        P("row", None, "col"),
        P(None, "row"),
        P(None, "col"),
    )
    return jax.shard_map(shards, mesh=mesh, in_specs=in_specs, out_specs=out_specs, check_vma=False)
```

```python
import functools

import jax
import jax.numpy as jnp
from jax import lax
from jax.experimental import pallas as pl
from jax.experimental.pallas import tpu as pltpu
from jax.sharding import PartitionSpec as P

D = 4096


def contract_tokens(left, right):
    return lax.dot_general(
        left, right, (((0,), (0,)), ((), ())), preferred_element_type=jnp.float32
    )


def pair_sum(part, axis, partner_bit, mine, scale):
    n = lax.axis_size("row")
    keep = lax.dynamic_index_in_dim(part, mine, axis, keepdims=False)
    give = lax.dynamic_index_in_dim(part, 1 - mine, axis, keepdims=False)
    got = lax.ppermute(
        (give * scale).astype(jnp.float16), "row", [(r, r ^ partner_bit) for r in range(n)]
    )
    return keep + got.astype(jnp.float32) / scale


def two_swaps(part, r, y_first, scale):
    y, z_lo, z_hi = r % 2, (r // 2) % 2, r // 4
    if y_first:
        part = pair_sum(part, 2, 1, y, scale)
        return pair_sum(part, 1, 2, z_lo, scale)
    part = pair_sum(part, 1, 2, z_lo, scale)
    return pair_sum(part, 0, 4, z_hi, scale)


def last_swap(part, r, y_first, scale):
    if y_first:
        return pair_sum(part, 0, 4, r // 4, scale)
    return pair_sum(part, 0, 1, r % 2, scale)


def gradient_rows(acts, flat_out):
    tok, width = acts.shape
    cols = flat_out.shape[1]
    r = lax.axis_index("row")
    top = lax.pmax(jnp.max(jnp.abs(flat_out)).astype(jnp.float32), "row")
    scale = 16384.0 / (6.0 * tok * lax.axis_size("row") * jnp.maximum(top, 1e-30))
    step = width // 4
    pieces = []
    sums = []
    for k in range(2):
        mine = acts.reshape(tok, 2, 2, step)[:, :, k].reshape(tok, 2 * step)
        full = lax.all_gather(mine, "col", axis=1, tiled=True)
        half = cols // 2
        if k == 1:
            full, *sums = lax.optimization_barrier((full, *sums))
            pieces.append([last_swap(sums[j], r, j == 0, scale) for j in range(2)])
        sums = []
        for j in range(2):
            part = contract_tokens(full, flat_out[:, j * half : (j + 1) * half])
            part = part.reshape(2, 2, 2, step, half)
            sums.append(two_swaps(part, r, j == 0, scale))
    pieces.append([last_swap(sums[j], r, j == 0, scale) for j in range(2)])
    return jnp.concatenate([jnp.concatenate(p, axis=1) for p in pieces], axis=0)


MESH = pl.DeviceIdType.MESH
CHUNK = 32


def exchange(axis, n, source, slots, send, recv):
    me = lax.axis_index(axis)

    def copy(to, slot):
        return pltpu.make_async_remote_copy(
            src_ref=source,
            dst_ref=slots.at[slot],
            send_sem=send.at[to],
            recv_sem=recv.at[slot],
            device_id={axis: to},
            device_id_type=MESH,
        )

    def start():
        for k in range(1, n):
            copy(lax.rem(me + k, n), me).start()
        slots[me] = source[...]

    def finish():
        for k in range(1, n):
            peer = lax.rem(me + k, n)
            copy(peer, peer).wait_recv()
        for k in range(1, n):
            copy(lax.rem(me + k, n), me).wait_send()

    return start, finish


def tail_kernel(
    rows_n, cols_n, grad, row_part, col_part, row_stat, col_stat, master,
    fresh, master_out, update, row_out, col_out,
    row_slots, col_slots, row_tall, pair, pair_slots, one, one_slots,
    rs, rr, cs, cr, ps, pr, os, orr, item_send, item_recv,
):
    r, c = lax.axis_index("row"), lax.axis_index("col")
    height, width = grad.shape
    y, z = lax.rem(r, 2), r // 2
    depth = rows_n // 2
    barrier = pltpu.get_barrier_semaphore()
    for k in range(1, rows_n):
        pl.semaphore_signal(barrier, inc=1, device_id={"row": lax.rem(r + k, rows_n)}, device_id_type=MESH)
    for k in range(1, cols_n):
        pl.semaphore_signal(barrier, inc=1, device_id={"col": lax.rem(c + k, cols_n)}, device_id_type=MESH)
    pl.semaphore_wait(barrier, rows_n + cols_n - 2)

    start_c, finish_c = exchange("row", rows_n, col_part, col_slots, cs, cr)
    start_r, finish_r = exchange("col", cols_n, row_part, row_slots, rs, rr)
    start_c()
    start_r()
    finish_r()
    new_row = 0.75 * row_stat[...] + 0.25 * jnp.sum(row_slots[...], axis=0) / D
    row_out[...] = new_row[0:1]
    row_tall[...] = jnp.transpose(jnp.broadcast_to(new_row[0:1], (128, height)))
    pair[8:16] = jnp.broadcast_to(jnp.sum(new_row, axis=1, keepdims=True), (8, 128))
    finish_c()
    new_col = 0.75 * col_stat[...] + 0.25 * jnp.sum(col_slots[...], axis=0) / D
    col_out[...] = new_col[0:1]

    def scaled(i, total):
        here = pl.ds(pl.multiple_of(i * CHUNK, CHUNK), CHUNK)
        value = grad[here] * lax.rsqrt(row_tall[here][:, 0:1] * col_out[...])
        update[here] = value
        return total + jnp.sum((value * value).reshape(CHUNK // 8, 8, width), axis=0)

    total = lax.fori_loop(0, height // CHUNK, scaled, jnp.zeros((8, width), jnp.float32))
    total = jnp.sum(jnp.sum(total, axis=0, keepdims=True), axis=1, keepdims=True)
    pair[0:8] = jnp.broadcast_to(total, (8, 128))
    start_p, finish_p = exchange("row", rows_n, pair, pair_slots, ps, pr)
    start_p()
    finish_p()
    both = jnp.sum(pair_slots[...], axis=0)
    one[...] = both[0:8]
    start_o, finish_o = exchange("col", cols_n, one, one_slots, os, orr)
    start_o()
    finish_o()
    mean = both[8:16] / D
    rms = jnp.sqrt(jnp.sum(one_slots[...], axis=0) * mean / (D * D))
    factor = (jnp.sqrt(mean) / jnp.maximum(1.0, rms))[0:1, 0:1]

    def finished(i, carry):
        here = pl.ds(pl.multiple_of(i * CHUNK, CHUNK), CHUNK)
        value = update[here] * factor
        update[here] = value
        value = master[here] - 0.01 * value
        master_out[here] = value
        fresh[pl.ds(pl.multiple_of(r * height + i * CHUNK, CHUNK), CHUNK)] = value.astype(jnp.bfloat16)
        return carry

    first = height * 3 // 16
    cuts = (0, first, (height + first) // 2, height)

    def item(zs, ys, half, way):
        number = (zs * 2 + ys) * 3 + half
        begins = pl.multiple_of((zs * 2 + ys) * height + cuts[half], 16)
        place = fresh.at[pl.ds(begins, cuts[half + 1] - cuts[half])]
        target = r + (1 - 2 * y) if way == 0 else (r + 2 if way == 1 else r - 2)
        return pltpu.make_async_remote_copy(
            src_ref=place,
            dst_ref=place,
            send_sem=item_send.at[number * 3 + way],
            recv_sem=item_recv.at[number],
            device_id={"row": target},
            device_id_type=MESH,
        )

    def along(zs, ys, half, way, act):
        @pl.when(z < depth - 1 if way == 1 else z > 0)
        def _():
            act(item(zs, ys, half, way))

    def begin(copy):
        copy.start()

    def sent(copy):
        copy.wait_send()

    def arrived(copy):
        copy.wait_recv()

    lax.fori_loop(0, cuts[1] // CHUNK, finished, 0)
    item(z, y, 0, 0).start()
    for way in (1, 2):
        along(z, y, 0, way, begin)
    lax.fori_loop(cuts[1] // CHUNK, height // CHUNK, finished, 0)
    for half in (1, 2):
        for way in (1, 2):
            along(z, y, half, way, begin)
        item(z, y, half, 0).start()
    item(z, 1 - y, 0, 0).wait_recv()
    for way in (1, 2):
        along(z, 1 - y, 0, way, begin)

    kinds = ((y, 0), (y, 1), (y, 2), (1 - y, 0))

    def each(k, way, do):
        zs = z - k if way == 1 else z + k

        @pl.when(zs >= 0 if way == 1 else zs < depth)
        def _():
            do(zs)

    for k in range(1, depth):
        for ys, half in kinds:
            for way in (1, 2):
                def pass_on(zs, ys=ys, half=half, way=way):
                    arrived(item(zs, ys, half, 0))
                    along(zs, ys, half, way, begin)
                    if half >= 1:
                        item(zs, ys, half, 0).start()

                each(k, way, pass_on)

    for k in range(depth):
        for way in (1, 2) if k else (1,):
            def last(zs):
                for half in (1, 2):
                    arrived(item(zs, 1 - y, half, 0))
                    sent(item(zs, y, half, 0))

            each(k, way, last)
    item(z, y, 0, 0).wait_send()
    for k in range(depth):
        for ys, half in kinds:
            for way in (1, 2):
                def drain(zs, ys=ys, half=half, way=way):
                    along(zs, ys, half, way, sent)

                each(k, way, drain)


def tail(grad, row_part, col_part, row_stat, col_stat, master):
    rows_n, cols_n = lax.axis_size("row"), lax.axis_size("col")
    height, width = grad.shape
    f32 = jnp.float32

    def eight(x):
        return jnp.broadcast_to(x, (8, x.shape[1]))

    vmem = pl.BlockSpec(memory_space=pltpu.VMEM)
    dma = pltpu.SemaphoreType.DMA
    items = rows_n * 3
    return pl.pallas_call(
        functools.partial(tail_kernel, rows_n, cols_n),
        out_shape=(
            jax.ShapeDtypeStruct((rows_n * height, width), jnp.bfloat16),
            jax.ShapeDtypeStruct((height, width), f32),
            jax.ShapeDtypeStruct((height, width), f32),
            jax.ShapeDtypeStruct((1, height), f32),
            jax.ShapeDtypeStruct((1, width), f32),
        ),
        in_specs=[vmem] * 6,
        out_specs=(vmem,) * 5,
        scratch_shapes=[
            pltpu.VMEM((cols_n, 8, height), f32),
            pltpu.VMEM((rows_n, 8, width), f32),
            pltpu.VMEM((height, 128), f32),
            pltpu.VMEM((16, 128), f32),
            pltpu.VMEM((rows_n, 16, 128), f32),
            pltpu.VMEM((8, 128), f32),
            pltpu.VMEM((cols_n, 8, 128), f32),
            dma((cols_n,)), dma((cols_n,)),
            dma((rows_n,)), dma((rows_n,)),
            dma((rows_n,)), dma((rows_n,)),
            dma((cols_n,)), dma((cols_n,)),
            dma((items * 3,)), dma((items,)),
        ],
        compiler_params=pltpu.CompilerParams(
            collective_id=0, has_side_effects=True, vmem_limit_bytes=40 * 1024 * 1024
        ),
    )(grad, eight(row_part), eight(col_part), eight(row_stat), eight(col_stat), master)


def shards(acts, out_grads, row_stat, col_stat, master):
    tok_here, mats, width_c = out_grads.shape
    flat_out = out_grads.reshape(tok_here, mats * width_c)
    rows_here = master.shape[0]
    if (lax.axis_size("row"), lax.axis_size("col"), mats) == (8, 4, 1):
        grad = gradient_rows(acts, flat_out)
        squares = grad * grad + 1e-30
        fresh, master_out, update_out, row_out, col_out = tail(
            grad,
            jnp.sum(squares, axis=1)[None],
            jnp.sum(squares, axis=0)[None],
            row_stat,
            col_stat,
            master.reshape(rows_here, width_c),
        )
        return (
            fresh.reshape(-1, mats, width_c),
            master_out.reshape(master.shape),
            update_out.reshape(master.shape),
            row_out,
            col_out,
        )
    else:
        acts_full = lax.all_gather(acts, "col", axis=1, tiled=True)
        grad = lax.psum_scatter(
            contract_tokens(acts_full, flat_out), "row", scatter_dimension=0, tiled=True
        )
    grad = grad.reshape(rows_here, mats, width_c)
    squares = grad * grad + 1e-30
    row_part = jnp.sum(squares, axis=2).T
    col_part = jnp.sum(squares, axis=0)
    row_sum = lax.psum(row_part, "col")
    row_out = 0.75 * row_stat + 0.25 * row_sum / D
    col_sum, row_total = lax.psum((col_part, jnp.sum(row_out, axis=1)), "row")
    col_out = 0.75 * col_stat + 0.25 * col_sum / D
    row_mean = row_total / D
    raw = grad * lax.rsqrt(row_out.T[:, :, None] * col_out[None, :, :] / row_mean[None, :, None])
    total_sq = lax.psum(jnp.sum(raw * raw, axis=(0, 2)), ("row", "col"))
    rms = jnp.sqrt(total_sq / (D * D))
    update_out = raw / jnp.maximum(1.0, rms)[None, :, None]
    master_out = master - 0.01 * update_out
    fresh = lax.all_gather(master_out.astype(jnp.bfloat16), "row", axis=0, tiled=True)
    return (fresh, master_out, update_out, row_out, col_out)


def solution(mesh):
    in_specs = (
        P("row", "col"),
        P("row", None, "col"),
        P(None, "row"),
        P(None, "col"),
        P("row", None, "col"),
    )
    out_specs = (
        P(None, None, "col"),
        P("row", None, "col"),
        P("row", None, "col"),
        P(None, "row"),
        P(None, "col"),
    )
    return jax.shard_map(shards, mesh=mesh, in_specs=in_specs, out_specs=out_specs, check_vma=False)
```

```python
import functools

import jax
import jax.numpy as jnp
from jax import lax
from jax.experimental import pallas as pl
from jax.experimental.pallas import tpu as pltpu
from jax.sharding import PartitionSpec as P

D = 4096


def contract_tokens(left, right):
    return lax.dot_general(
        left, right, (((0,), (0,)), ((), ())), preferred_element_type=jnp.float32
    )


def pair_sum(part, axis, partner_bit, mine, scale):
    n = lax.axis_size("row")
    keep = lax.dynamic_index_in_dim(part, mine, axis, keepdims=False)
    give = lax.dynamic_index_in_dim(part, 1 - mine, axis, keepdims=False)
    got = lax.ppermute(
        (give * scale).astype(jnp.float16), "row", [(r, r ^ partner_bit) for r in range(n)]
    )
    return keep + got.astype(jnp.float32) / scale


def two_swaps(part, r, y_first, scale):
    y, z_lo, z_hi = r % 2, (r // 2) % 2, r // 4
    if y_first:
        part = pair_sum(part, 2, 1, y, scale)
        return pair_sum(part, 1, 2, z_lo, scale)
    part = pair_sum(part, 1, 2, z_lo, scale)
    return pair_sum(part, 0, 4, z_hi, scale)


def last_swap(part, r, y_first, scale):
    if y_first:
        return pair_sum(part, 0, 4, r // 4, scale)
    return pair_sum(part, 0, 1, r % 2, scale)


def gradient_rows(acts, flat_out):
    tok, width = acts.shape
    cols = flat_out.shape[1]
    r = lax.axis_index("row")
    top = lax.pmax(jnp.max(jnp.abs(flat_out)).astype(jnp.float32), "row")
    scale = 16384.0 / (6.0 * tok * lax.axis_size("row") * jnp.maximum(top, 1e-30))
    step = width // 4
    pieces = []
    sums = []
    for k in range(2):
        mine = acts.reshape(tok, 2, 2, step)[:, :, k].reshape(tok, 2 * step)
        full = lax.all_gather(mine, "col", axis=1, tiled=True)
        half = cols // 2
        if k == 1:
            full, sums[0] = lax.optimization_barrier((full, sums[0]))
            pieces.append([last_swap(sums[j], r, j == 0, scale) for j in range(2)])
        sums = []
        for j in range(2):
            part = contract_tokens(full, flat_out[:, j * half : (j + 1) * half])
            part = part.reshape(2, 2, 2, step, half)
            sums.append(two_swaps(part, r, j == 0, scale))
    pieces.append([last_swap(sums[j], r, j == 0, scale) for j in range(2)])
    return jnp.concatenate([jnp.concatenate(p, axis=1) for p in pieces], axis=0)


MESH = pl.DeviceIdType.MESH
CHUNK = 32


def exchange(axis, n, source, slots, send, recv):
    me = lax.axis_index(axis)

    def copy(to, slot):
        return pltpu.make_async_remote_copy(
            src_ref=source,
            dst_ref=slots.at[slot],
            send_sem=send.at[to],
            recv_sem=recv.at[slot],
            device_id={axis: to},
            device_id_type=MESH,
        )

    def start():
        for k in range(1, n):
            copy(lax.rem(me + k, n), me).start()
        slots[me] = source[...]

    def finish():
        for k in range(1, n):
            peer = lax.rem(me + k, n)
            copy(peer, peer).wait_recv()
        for k in range(1, n):
            copy(lax.rem(me + k, n), me).wait_send()

    return start, finish


def tail_kernel(
    rows_n, cols_n, grad, row_part, col_part, row_stat, col_stat, master,
    fresh, master_out, update, row_out, col_out,
    row_slots, col_slots, row_tall, pair, pair_slots, one, one_slots,
    rs, rr, cs, cr, ps, pr, os, orr, item_send, item_recv,
):
    r, c = lax.axis_index("row"), lax.axis_index("col")
    height, width = grad.shape
    y, z = lax.rem(r, 2), r // 2
    depth = rows_n // 2
    barrier = pltpu.get_barrier_semaphore()
    for k in range(1, rows_n):
        pl.semaphore_signal(barrier, inc=1, device_id={"row": lax.rem(r + k, rows_n)}, device_id_type=MESH)
    for k in range(1, cols_n):
        pl.semaphore_signal(barrier, inc=1, device_id={"col": lax.rem(c + k, cols_n)}, device_id_type=MESH)
    pl.semaphore_wait(barrier, rows_n + cols_n - 2)

    start_c, finish_c = exchange("row", rows_n, col_part, col_slots, cs, cr)
    start_r, finish_r = exchange("col", cols_n, row_part, row_slots, rs, rr)
    start_c()
    start_r()
    finish_r()
    new_row = 0.75 * row_stat[...] + 0.25 * jnp.sum(row_slots[...], axis=0) / D
    row_out[...] = new_row[0:1]
    row_tall[...] = jnp.transpose(jnp.broadcast_to(new_row[0:1], (128, height)))
    pair[8:16] = jnp.broadcast_to(jnp.sum(new_row, axis=1, keepdims=True), (8, 128))
    finish_c()
    new_col = 0.75 * col_stat[...] + 0.25 * jnp.sum(col_slots[...], axis=0) / D
    col_out[...] = new_col[0:1]

    def scaled(i, total):
        here = pl.ds(pl.multiple_of(i * CHUNK, CHUNK), CHUNK)
        value = grad[here] * lax.rsqrt(row_tall[here][:, 0:1] * col_out[...])
        update[here] = value
        return total + jnp.sum((value * value).reshape(CHUNK // 8, 8, width), axis=0)

    total = lax.fori_loop(0, height // CHUNK, scaled, jnp.zeros((8, width), jnp.float32))
    total = jnp.sum(jnp.sum(total, axis=0, keepdims=True), axis=1, keepdims=True)
    pair[0:8] = jnp.broadcast_to(total, (8, 128))
    start_p, finish_p = exchange("row", rows_n, pair, pair_slots, ps, pr)
    start_p()
    finish_p()
    both = jnp.sum(pair_slots[...], axis=0)
    one[...] = both[0:8]
    start_o, finish_o = exchange("col", cols_n, one, one_slots, os, orr)
    start_o()
    finish_o()
    mean = both[8:16] / D
    rms = jnp.sqrt(jnp.sum(one_slots[...], axis=0) * mean / (D * D))
    factor = (jnp.sqrt(mean) / jnp.maximum(1.0, rms))[0:1, 0:1]

    def finished(i, carry):
        here = pl.ds(pl.multiple_of(i * CHUNK, CHUNK), CHUNK)
        value = update[here] * factor
        update[here] = value
        value = master[here] - 0.01 * value
        master_out[here] = value
        fresh[pl.ds(pl.multiple_of(r * height + i * CHUNK, CHUNK), CHUNK)] = value.astype(jnp.bfloat16)
        return carry

    first = height * 3 // 16
    cuts = (0, first, (height + first) // 2, height)

    def item(zs, ys, half, way):
        number = (zs * 2 + ys) * 3 + half
        begins = pl.multiple_of((zs * 2 + ys) * height + cuts[half], 16)
        place = fresh.at[pl.ds(begins, cuts[half + 1] - cuts[half])]
        target = r + (1 - 2 * y) if way == 0 else (r + 2 if way == 1 else r - 2)
        return pltpu.make_async_remote_copy(
            src_ref=place,
            dst_ref=place,
            send_sem=item_send.at[number * 3 + way],
            recv_sem=item_recv.at[number],
            device_id={"row": target},
            device_id_type=MESH,
        )

    def along(zs, ys, half, way, act):
        @pl.when(z < depth - 1 if way == 1 else z > 0)
        def _():
            act(item(zs, ys, half, way))

    def begin(copy):
        copy.start()

    def sent(copy):
        copy.wait_send()

    def arrived(copy):
        copy.wait_recv()

    lax.fori_loop(0, cuts[1] // CHUNK, finished, 0)
    item(z, y, 0, 0).start()
    for way in (1, 2):
        along(z, y, 0, way, begin)
    lax.fori_loop(cuts[1] // CHUNK, height // CHUNK, finished, 0)
    for half in (1, 2):
        for way in (1, 2):
            along(z, y, half, way, begin)
        item(z, y, half, 0).start()
    item(z, 1 - y, 0, 0).wait_recv()
    for way in (1, 2):
        along(z, 1 - y, 0, way, begin)

    kinds = ((y, 0), (y, 1), (y, 2), (1 - y, 0))

    def each(k, way, do):
        zs = z - k if way == 1 else z + k

        @pl.when(zs >= 0 if way == 1 else zs < depth)
        def _():
            do(zs)

    for k in range(1, depth):
        for ys, half in kinds:
            for way in (1, 2):
                def pass_on(zs, ys=ys, half=half, way=way):
                    arrived(item(zs, ys, half, 0))
                    along(zs, ys, half, way, begin)
                    if half >= 1:
                        item(zs, ys, half, 0).start()

                each(k, way, pass_on)

    for k in range(depth):
        for way in (1, 2) if k else (1,):
            def last(zs):
                for half in (1, 2):
                    arrived(item(zs, 1 - y, half, 0))
                    sent(item(zs, y, half, 0))

            each(k, way, last)
    item(z, y, 0, 0).wait_send()
    for k in range(depth):
        for ys, half in kinds:
            for way in (1, 2):
                def drain(zs, ys=ys, half=half, way=way):
                    along(zs, ys, half, way, sent)

                each(k, way, drain)


def tail(grad, row_part, col_part, row_stat, col_stat, master):
    rows_n, cols_n = lax.axis_size("row"), lax.axis_size("col")
    height, width = grad.shape
    f32 = jnp.float32

    def eight(x):
        return jnp.broadcast_to(x, (8, x.shape[1]))

    vmem = pl.BlockSpec(memory_space=pltpu.VMEM)
    dma = pltpu.SemaphoreType.DMA
    items = rows_n * 3
    return pl.pallas_call(
        functools.partial(tail_kernel, rows_n, cols_n),
        out_shape=(
            jax.ShapeDtypeStruct((rows_n * height, width), jnp.bfloat16),
            jax.ShapeDtypeStruct((height, width), f32),
            jax.ShapeDtypeStruct((height, width), f32),
            jax.ShapeDtypeStruct((1, height), f32),
            jax.ShapeDtypeStruct((1, width), f32),
        ),
        in_specs=[vmem] * 6,
        out_specs=(vmem,) * 5,
        scratch_shapes=[
            pltpu.VMEM((cols_n, 8, height), f32),
            pltpu.VMEM((rows_n, 8, width), f32),
            pltpu.VMEM((height, 128), f32),
            pltpu.VMEM((16, 128), f32),
            pltpu.VMEM((rows_n, 16, 128), f32),
            pltpu.VMEM((8, 128), f32),
            pltpu.VMEM((cols_n, 8, 128), f32),
            dma((cols_n,)), dma((cols_n,)),
            dma((rows_n,)), dma((rows_n,)),
            dma((rows_n,)), dma((rows_n,)),
            dma((cols_n,)), dma((cols_n,)),
            dma((items * 3,)), dma((items,)),
        ],
        compiler_params=pltpu.CompilerParams(
            collective_id=0, has_side_effects=True, vmem_limit_bytes=40 * 1024 * 1024
        ),
    )(grad, eight(row_part), eight(col_part), eight(row_stat), eight(col_stat), master)


def shards(acts, out_grads, row_stat, col_stat, master):
    tok_here, mats, width_c = out_grads.shape
    flat_out = out_grads.reshape(tok_here, mats * width_c)
    rows_here = master.shape[0]
    if (lax.axis_size("row"), lax.axis_size("col"), mats) == (8, 4, 1):
        grad = gradient_rows(acts, flat_out)
        squares = grad * grad + 1e-30
        fresh, master_out, update_out, row_out, col_out = tail(
            grad,
            jnp.sum(squares, axis=1)[None],
            jnp.sum(squares, axis=0)[None],
            row_stat,
            col_stat,
            master.reshape(rows_here, width_c),
        )
        return (
            fresh.reshape(-1, mats, width_c),
            master_out.reshape(master.shape),
            update_out.reshape(master.shape),
            row_out,
            col_out,
        )
    else:
        acts_full = lax.all_gather(acts, "col", axis=1, tiled=True)
        grad = lax.psum_scatter(
            contract_tokens(acts_full, flat_out), "row", scatter_dimension=0, tiled=True
        )
    grad = grad.reshape(rows_here, mats, width_c)
    squares = grad * grad + 1e-30
    row_part = jnp.sum(squares, axis=2).T
    col_part = jnp.sum(squares, axis=0)
    row_sum = lax.psum(row_part, "col")
    row_out = 0.75 * row_stat + 0.25 * row_sum / D
    col_sum, row_total = lax.psum((col_part, jnp.sum(row_out, axis=1)), "row")
    col_out = 0.75 * col_stat + 0.25 * col_sum / D
    row_mean = row_total / D
    raw = grad * lax.rsqrt(row_out.T[:, :, None] * col_out[None, :, :] / row_mean[None, :, None])
    total_sq = lax.psum(jnp.sum(raw * raw, axis=(0, 2)), ("row", "col"))
    rms = jnp.sqrt(total_sq / (D * D))
    update_out = raw / jnp.maximum(1.0, rms)[None, :, None]
    master_out = master - 0.01 * update_out
    fresh = lax.all_gather(master_out.astype(jnp.bfloat16), "row", axis=0, tiled=True)
    return (fresh, master_out, update_out, row_out, col_out)


def solution(mesh):
    in_specs = (
        P("row", "col"),
        P("row", None, "col"),
        P(None, "row"),
        P(None, "col"),
        P("row", None, "col"),
    )
    out_specs = (
        P(None, None, "col"),
        P("row", None, "col"),
        P("row", None, "col"),
        P(None, "row"),
        P(None, "col"),
    )
    return jax.shard_map(shards, mesh=mesh, in_specs=in_specs, out_specs=out_specs, check_vma=False)
```

```python
import functools

import jax
import jax.numpy as jnp
from jax import lax
from jax.experimental import pallas as pl
from jax.experimental.pallas import tpu as pltpu
from jax.sharding import PartitionSpec as P

D = 4096


def contract_tokens(left, right):
    return lax.dot_general(
        left, right, (((0,), (0,)), ((), ())), preferred_element_type=jnp.float32
    )


def pair_sum(part, axis, partner_bit, mine, scale):
    n = lax.axis_size("row")
    keep = lax.dynamic_index_in_dim(part, mine, axis, keepdims=False)
    give = lax.dynamic_index_in_dim(part, 1 - mine, axis, keepdims=False)
    got = lax.ppermute(
        (give * scale).astype(jnp.float16), "row", [(r, r ^ partner_bit) for r in range(n)]
    )
    return keep + got.astype(jnp.float32) / scale


def two_swaps(part, r, y_first, scale):
    y, z_lo, z_hi = r % 2, (r // 2) % 2, r // 4
    if y_first:
        part = pair_sum(part, 2, 1, y, scale)
        return pair_sum(part, 1, 2, z_lo, scale)
    part = pair_sum(part, 1, 2, z_lo, scale)
    return pair_sum(part, 0, 4, z_hi, scale)


def last_swap(part, r, y_first, scale):
    if y_first:
        return pair_sum(part, 0, 4, r // 4, scale)
    return pair_sum(part, 0, 1, r % 2, scale)


def gradient_rows(acts, flat_out):
    tok, width = acts.shape
    cols = flat_out.shape[1]
    r = lax.axis_index("row")
    top = lax.pmax(jnp.max(jnp.abs(flat_out)).astype(jnp.float32), "row")
    scale = 16384.0 / (6.0 * tok * lax.axis_size("row") * jnp.maximum(top, 1e-30))
    parts = 4
    step = width // (2 * parts)
    pieces = []
    sums = []
    for k in range(parts):
        mine = acts.reshape(tok, 2, parts, step)[:, :, k].reshape(tok, 2 * step)
        full = lax.all_gather(mine, "col", axis=1, tiled=True)
        half = cols // 2
        if k:
            full, sums[0] = lax.optimization_barrier((full, sums[0]))
            pieces.append([last_swap(sums[j], r, j == 0, scale) for j in range(2)])
        sums = []
        for j in range(2):
            part = contract_tokens(full, flat_out[:, j * half : (j + 1) * half])
            part = part.reshape(2, 2, 2, step, half)
            sums.append(two_swaps(part, r, j == 0, scale))
    pieces.append([last_swap(sums[j], r, j == 0, scale) for j in range(2)])
    return jnp.concatenate([jnp.concatenate(p, axis=1) for p in pieces], axis=0)


MESH = pl.DeviceIdType.MESH
CHUNK = 32


def exchange(axis, n, source, slots, send, recv):
    me = lax.axis_index(axis)

    def copy(to, slot):
        return pltpu.make_async_remote_copy(
            src_ref=source,
            dst_ref=slots.at[slot],
            send_sem=send.at[to],
            recv_sem=recv.at[slot],
            device_id={axis: to},
            device_id_type=MESH,
        )

    def start():
        for k in range(1, n):
            copy(lax.rem(me + k, n), me).start()
        slots[me] = source[...]

    def finish():
        for k in range(1, n):
            peer = lax.rem(me + k, n)
            copy(peer, peer).wait_recv()
        for k in range(1, n):
            copy(lax.rem(me + k, n), me).wait_send()

    return start, finish


def tail_kernel(
    rows_n, cols_n, grad, row_part, col_part, row_stat, col_stat, master,
    fresh, master_out, update, row_out, col_out,
    row_slots, col_slots, row_tall, pair, pair_slots, one, one_slots,
    rs, rr, cs, cr, ps, pr, os, orr, item_send, item_recv,
):
    r, c = lax.axis_index("row"), lax.axis_index("col")
    height, width = grad.shape
    y, z = lax.rem(r, 2), r // 2
    depth = rows_n // 2
    barrier = pltpu.get_barrier_semaphore()
    for k in range(1, rows_n):
        pl.semaphore_signal(barrier, inc=1, device_id={"row": lax.rem(r + k, rows_n)}, device_id_type=MESH)
    for k in range(1, cols_n):
        pl.semaphore_signal(barrier, inc=1, device_id={"col": lax.rem(c + k, cols_n)}, device_id_type=MESH)
    pl.semaphore_wait(barrier, rows_n + cols_n - 2)

    start_c, finish_c = exchange("row", rows_n, col_part, col_slots, cs, cr)
    start_r, finish_r = exchange("col", cols_n, row_part, row_slots, rs, rr)
    start_c()
    start_r()
    finish_r()
    new_row = 0.75 * row_stat[...] + 0.25 * jnp.sum(row_slots[...], axis=0) / D
    row_out[...] = new_row[0:1]
    row_tall[...] = jnp.transpose(jnp.broadcast_to(new_row[0:1], (128, height)))
    pair[8:16] = jnp.broadcast_to(jnp.sum(new_row, axis=1, keepdims=True), (8, 128))
    finish_c()
    new_col = 0.75 * col_stat[...] + 0.25 * jnp.sum(col_slots[...], axis=0) / D
    col_out[...] = new_col[0:1]

    def scaled(i, total):
        here = pl.ds(pl.multiple_of(i * CHUNK, CHUNK), CHUNK)
        value = grad[here] * lax.rsqrt(row_tall[here][:, 0:1] * col_out[...])
        update[here] = value
        return total + jnp.sum((value * value).reshape(CHUNK // 8, 8, width), axis=0)

    total = lax.fori_loop(0, height // CHUNK, scaled, jnp.zeros((8, width), jnp.float32))
    total = jnp.sum(jnp.sum(total, axis=0, keepdims=True), axis=1, keepdims=True)
    pair[0:8] = jnp.broadcast_to(total, (8, 128))
    start_p, finish_p = exchange("row", rows_n, pair, pair_slots, ps, pr)
    start_p()
    finish_p()
    both = jnp.sum(pair_slots[...], axis=0)
    one[...] = both[0:8]
    start_o, finish_o = exchange("col", cols_n, one, one_slots, os, orr)
    start_o()
    finish_o()
    mean = both[8:16] / D
    rms = jnp.sqrt(jnp.sum(one_slots[...], axis=0) * mean / (D * D))
    factor = (jnp.sqrt(mean) / jnp.maximum(1.0, rms))[0:1, 0:1]

    def finished(i, carry):
        here = pl.ds(pl.multiple_of(i * CHUNK, CHUNK), CHUNK)
        value = update[here] * factor
        update[here] = value
        value = master[here] - 0.01 * value
        master_out[here] = value
        fresh[pl.ds(pl.multiple_of(r * height + i * CHUNK, CHUNK), CHUNK)] = value.astype(jnp.bfloat16)
        return carry

    first = height * 3 // 16
    cuts = (0, first, (height + first) // 2, height)

    def item(zs, ys, half, way):
        number = (zs * 2 + ys) * 3 + half
        begins = pl.multiple_of((zs * 2 + ys) * height + cuts[half], 16)
        place = fresh.at[pl.ds(begins, cuts[half + 1] - cuts[half])]
        target = r + (1 - 2 * y) if way == 0 else (r + 2 if way == 1 else r - 2)
        return pltpu.make_async_remote_copy(
            src_ref=place,
            dst_ref=place,
            send_sem=item_send.at[number * 3 + way],
            recv_sem=item_recv.at[number],
            device_id={"row": target},
            device_id_type=MESH,
        )

    def along(zs, ys, half, way, act):
        @pl.when(z < depth - 1 if way == 1 else z > 0)
        def _():
            act(item(zs, ys, half, way))

    def begin(copy):
        copy.start()

    def sent(copy):
        copy.wait_send()

    def arrived(copy):
        copy.wait_recv()

    lax.fori_loop(0, cuts[1] // CHUNK, finished, 0)
    item(z, y, 0, 0).start()
    for way in (1, 2):
        along(z, y, 0, way, begin)
    lax.fori_loop(cuts[1] // CHUNK, height // CHUNK, finished, 0)
    for half in (1, 2):
        for way in (1, 2):
            along(z, y, half, way, begin)
        item(z, y, half, 0).start()
    item(z, 1 - y, 0, 0).wait_recv()
    for way in (1, 2):
        along(z, 1 - y, 0, way, begin)

    kinds = ((y, 0), (y, 1), (y, 2), (1 - y, 0))

    def each(k, way, do):
        zs = z - k if way == 1 else z + k

        @pl.when(zs >= 0 if way == 1 else zs < depth)
        def _():
            do(zs)

    for k in range(1, depth):
        for ys, half in kinds:
            for way in (1, 2):
                def pass_on(zs, ys=ys, half=half, way=way):
                    arrived(item(zs, ys, half, 0))
                    along(zs, ys, half, way, begin)
                    if half >= 1:
                        item(zs, ys, half, 0).start()

                each(k, way, pass_on)

    for k in range(depth):
        for way in (1, 2) if k else (1,):
            def last(zs):
                for half in (1, 2):
                    arrived(item(zs, 1 - y, half, 0))
                    sent(item(zs, y, half, 0))

            each(k, way, last)
    item(z, y, 0, 0).wait_send()
    for k in range(depth):
        for ys, half in kinds:
            for way in (1, 2):
                def drain(zs, ys=ys, half=half, way=way):
                    along(zs, ys, half, way, sent)

                each(k, way, drain)


def tail(grad, row_part, col_part, row_stat, col_stat, master):
    rows_n, cols_n = lax.axis_size("row"), lax.axis_size("col")
    height, width = grad.shape
    f32 = jnp.float32

    def eight(x):
        return jnp.broadcast_to(x, (8, x.shape[1]))

    vmem = pl.BlockSpec(memory_space=pltpu.VMEM)
    dma = pltpu.SemaphoreType.DMA
    items = rows_n * 3
    return pl.pallas_call(
        functools.partial(tail_kernel, rows_n, cols_n),
        out_shape=(
            jax.ShapeDtypeStruct((rows_n * height, width), jnp.bfloat16),
            jax.ShapeDtypeStruct((height, width), f32),
            jax.ShapeDtypeStruct((height, width), f32),
            jax.ShapeDtypeStruct((1, height), f32),
            jax.ShapeDtypeStruct((1, width), f32),
        ),
        in_specs=[vmem] * 6,
        out_specs=(vmem,) * 5,
        scratch_shapes=[
            pltpu.VMEM((cols_n, 8, height), f32),
            pltpu.VMEM((rows_n, 8, width), f32),
            pltpu.VMEM((height, 128), f32),
            pltpu.VMEM((16, 128), f32),
            pltpu.VMEM((rows_n, 16, 128), f32),
            pltpu.VMEM((8, 128), f32),
            pltpu.VMEM((cols_n, 8, 128), f32),
            dma((cols_n,)), dma((cols_n,)),
            dma((rows_n,)), dma((rows_n,)),
            dma((rows_n,)), dma((rows_n,)),
            dma((cols_n,)), dma((cols_n,)),
            dma((items * 3,)), dma((items,)),
        ],
        compiler_params=pltpu.CompilerParams(
            collective_id=0, has_side_effects=True, vmem_limit_bytes=40 * 1024 * 1024
        ),
    )(grad, eight(row_part), eight(col_part), eight(row_stat), eight(col_stat), master)


def shards(acts, out_grads, row_stat, col_stat, master):
    tok_here, mats, width_c = out_grads.shape
    flat_out = out_grads.reshape(tok_here, mats * width_c)
    rows_here = master.shape[0]
    if (lax.axis_size("row"), lax.axis_size("col"), mats) == (8, 4, 1):
        grad = gradient_rows(acts, flat_out)
        squares = grad * grad + 1e-30
        fresh, master_out, update_out, row_out, col_out = tail(
            grad,
            jnp.sum(squares, axis=1)[None],
            jnp.sum(squares, axis=0)[None],
            row_stat,
            col_stat,
            master.reshape(rows_here, width_c),
        )
        return (
            fresh.reshape(-1, mats, width_c),
            master_out.reshape(master.shape),
            update_out.reshape(master.shape),
            row_out,
            col_out,
        )
    else:
        acts_full = lax.all_gather(acts, "col", axis=1, tiled=True)
        grad = lax.psum_scatter(
            contract_tokens(acts_full, flat_out), "row", scatter_dimension=0, tiled=True
        )
    grad = grad.reshape(rows_here, mats, width_c)
    squares = grad * grad + 1e-30
    row_part = jnp.sum(squares, axis=2).T
    col_part = jnp.sum(squares, axis=0)
    row_sum = lax.psum(row_part, "col")
    row_out = 0.75 * row_stat + 0.25 * row_sum / D
    col_sum, row_total = lax.psum((col_part, jnp.sum(row_out, axis=1)), "row")
    col_out = 0.75 * col_stat + 0.25 * col_sum / D
    row_mean = row_total / D
    raw = grad * lax.rsqrt(row_out.T[:, :, None] * col_out[None, :, :] / row_mean[None, :, None])
    total_sq = lax.psum(jnp.sum(raw * raw, axis=(0, 2)), ("row", "col"))
    rms = jnp.sqrt(total_sq / (D * D))
    update_out = raw / jnp.maximum(1.0, rms)[None, :, None]
    master_out = master - 0.01 * update_out
    fresh = lax.all_gather(master_out.astype(jnp.bfloat16), "row", axis=0, tiled=True)
    return (fresh, master_out, update_out, row_out, col_out)


def solution(mesh):
    in_specs = (
        P("row", "col"),
        P("row", None, "col"),
        P(None, "row"),
        P(None, "col"),
        P("row", None, "col"),
    )
    out_specs = (
        P(None, None, "col"),
        P("row", None, "col"),
        P("row", None, "col"),
        P(None, "row"),
        P(None, "col"),
    )
    return jax.shard_map(shards, mesh=mesh, in_specs=in_specs, out_specs=out_specs, check_vma=False)
```

```python
import functools

import jax
import jax.numpy as jnp
from jax import lax
from jax.experimental import pallas as pl
from jax.experimental.pallas import tpu as pltpu
from jax.sharding import PartitionSpec as P

D = 4096


def contract_tokens(left, right):
    return lax.dot_general(
        left, right, (((0,), (0,)), ((), ())), preferred_element_type=jnp.float32
    )


def pair_sum(part, axis, partner_bit, mine, scale):
    n = lax.axis_size("row")
    keep = lax.dynamic_index_in_dim(part, mine, axis, keepdims=False)
    give = lax.dynamic_index_in_dim(part, 1 - mine, axis, keepdims=False)
    got = lax.ppermute(
        (give * scale).astype(jnp.float16), "row", [(r, r ^ partner_bit) for r in range(n)]
    )
    return keep + got.astype(jnp.float32) / scale


def two_swaps(part, r, y_first, scale):
    y, z_lo, z_hi = r % 2, (r // 2) % 2, r // 4
    if y_first:
        part = pair_sum(part, 2, 1, y, scale)
        return pair_sum(part, 1, 2, z_lo, scale)
    part = pair_sum(part, 1, 2, z_lo, scale)
    return pair_sum(part, 0, 4, z_hi, scale)


def last_swap(part, r, y_first, scale):
    if y_first:
        return pair_sum(part, 0, 4, r // 4, scale)
    return pair_sum(part, 0, 1, r % 2, scale)


def gradient_rows(acts, flat_out):
    tok, width = acts.shape
    cols = flat_out.shape[1]
    r = lax.axis_index("row")
    top = lax.pmax(jnp.max(jnp.abs(flat_out)).astype(jnp.float32), "row")
    scale = 16384.0 / (6.0 * tok * lax.axis_size("row") * jnp.maximum(top, 1e-30))
    parts = 4
    step = width // (2 * parts)
    pieces = []
    sums = []
    for k in range(parts):
        mine = acts.reshape(tok, 2, parts, step)[:, :, k].reshape(tok, 2 * step)
        full = lax.all_gather(mine, "col", axis=1, tiled=True)
        half = cols // 2
        if k:
            full, sums[0] = lax.optimization_barrier((full, sums[0]))
            pieces.append([last_swap(sums[j], r, j == 0, scale) for j in range(2)])
        sums = []
        for j in range(2):
            part = contract_tokens(full, flat_out[:, j * half : (j + 1) * half])
            part = part.reshape(2, 2, 2, step, half)
            sums.append(two_swaps(part, r, j == 0, scale))
    pieces.append([last_swap(sums[j], r, j == 0, scale) for j in range(2)])
    return jnp.concatenate([jnp.concatenate(p, axis=1) for p in pieces], axis=0)


MESH = pl.DeviceIdType.MESH
CHUNK = 16


def exchange(axis, n, source, slots, send, recv):
    me = lax.axis_index(axis)

    def copy(to, slot):
        return pltpu.make_async_remote_copy(
            src_ref=source,
            dst_ref=slots.at[slot],
            send_sem=send.at[to],
            recv_sem=recv.at[slot],
            device_id={axis: to},
            device_id_type=MESH,
        )

    def start():
        for k in range(1, n):
            copy(lax.rem(me + k, n), me).start()
        slots[me] = source[...]

    def finish():
        for k in range(1, n):
            peer = lax.rem(me + k, n)
            copy(peer, peer).wait_recv()
        for k in range(1, n):
            copy(lax.rem(me + k, n), me).wait_send()

    return start, finish


def tail_kernel(
    rows_n, cols_n, grad, row_part, col_part, row_stat, col_stat, master,
    fresh, master_out, update, row_out, col_out,
    row_slots, col_slots, row_tall, pair, pair_slots, one, one_slots,
    rs, rr, cs, cr, ps, pr, os, orr, item_send, item_recv,
):
    r, c = lax.axis_index("row"), lax.axis_index("col")
    height, width = grad.shape
    y, z = lax.rem(r, 2), r // 2
    depth = rows_n // 2
    barrier = pltpu.get_barrier_semaphore()
    for k in range(1, rows_n):
        pl.semaphore_signal(barrier, inc=1, device_id={"row": lax.rem(r + k, rows_n)}, device_id_type=MESH)
    for k in range(1, cols_n):
        pl.semaphore_signal(barrier, inc=1, device_id={"col": lax.rem(c + k, cols_n)}, device_id_type=MESH)
    pl.semaphore_wait(barrier, rows_n + cols_n - 2)

    start_c, finish_c = exchange("row", rows_n, col_part, col_slots, cs, cr)
    start_r, finish_r = exchange("col", cols_n, row_part, row_slots, rs, rr)
    start_c()
    start_r()
    finish_r()
    new_row = 0.75 * row_stat[...] + 0.25 * jnp.sum(row_slots[...], axis=0) / D
    row_out[...] = new_row[0:1]
    row_tall[...] = jnp.transpose(jnp.broadcast_to(new_row[0:1], (128, height)))
    pair[8:16] = jnp.broadcast_to(jnp.sum(new_row, axis=1, keepdims=True), (8, 128))
    finish_c()
    new_col = 0.75 * col_stat[...] + 0.25 * jnp.sum(col_slots[...], axis=0) / D
    col_out[...] = new_col[0:1]

    def scaled(i, total):
        here = pl.ds(pl.multiple_of(i * CHUNK, CHUNK), CHUNK)
        value = grad[here] * lax.rsqrt(row_tall[here][:, 0:1] * col_out[...])
        update[here] = value
        return total + jnp.sum((value * value).reshape(CHUNK // 8, 8, width), axis=0)

    total = lax.fori_loop(0, height // CHUNK, scaled, jnp.zeros((8, width), jnp.float32))
    total = jnp.sum(jnp.sum(total, axis=0, keepdims=True), axis=1, keepdims=True)
    pair[0:8] = jnp.broadcast_to(total, (8, 128))
    start_p, finish_p = exchange("row", rows_n, pair, pair_slots, ps, pr)
    start_p()
    finish_p()
    both = jnp.sum(pair_slots[...], axis=0)
    one[...] = both[0:8]
    start_o, finish_o = exchange("col", cols_n, one, one_slots, os, orr)
    start_o()
    finish_o()
    mean = both[8:16] / D
    rms = jnp.sqrt(jnp.sum(one_slots[...], axis=0) * mean / (D * D))
    factor = (jnp.sqrt(mean) / jnp.maximum(1.0, rms))[0:1, 0:1]

    def finished(i, carry):
        here = pl.ds(pl.multiple_of(i * CHUNK, CHUNK), CHUNK)
        value = update[here] * factor
        update[here] = value
        value = master[here] - 0.01 * value
        master_out[here] = value
        fresh[pl.ds(pl.multiple_of(r * height + i * CHUNK, CHUNK), CHUNK)] = value.astype(jnp.bfloat16)
        return carry

    first = height * 3 // 16
    cuts = (0, first, height * 13 // 32, height * 5 // 8, height * 13 // 16, height)

    def item(zs, ys, half, way):
        number = (zs * 2 + ys) * 5 + half
        begins = pl.multiple_of((zs * 2 + ys) * height + cuts[half], 16)
        place = fresh.at[pl.ds(begins, cuts[half + 1] - cuts[half])]
        target = r + (1 - 2 * y) if way == 0 else (r + 2 if way == 1 else r - 2)
        return pltpu.make_async_remote_copy(
            src_ref=place,
            dst_ref=place,
            send_sem=item_send.at[number * 3 + way],
            recv_sem=item_recv.at[number],
            device_id={"row": target},
            device_id_type=MESH,
        )

    def along(zs, ys, half, way, act):
        @pl.when(z < depth - 1 if way == 1 else z > 0)
        def _():
            act(item(zs, ys, half, way))

    def begin(copy):
        copy.start()

    def sent(copy):
        copy.wait_send()

    def arrived(copy):
        copy.wait_recv()

    lax.fori_loop(0, cuts[1] // CHUNK, finished, 0)
    item(z, y, 0, 0).start()
    for way in (1, 2):
        along(z, y, 0, way, begin)
    for half in range(1, 5):
        lax.fori_loop(cuts[half] // CHUNK, cuts[half + 1] // CHUNK, finished, 0)
        for way in (1, 2):
            along(z, y, half, way, begin)
        item(z, y, half, 0).start()
    item(z, 1 - y, 0, 0).wait_recv()
    for way in (1, 2):
        along(z, 1 - y, 0, way, begin)

    kinds = ((y, 0), (y, 1), (y, 2), (y, 3), (y, 4), (1 - y, 0))

    def each(k, way, do):
        zs = z - k if way == 1 else z + k

        @pl.when(zs >= 0 if way == 1 else zs < depth)
        def _():
            do(zs)

    for k in range(1, depth):
        for ys, half in kinds:
            for way in (1, 2):
                def pass_on(zs, ys=ys, half=half, way=way):
                    arrived(item(zs, ys, half, 0))
                    along(zs, ys, half, way, begin)
                    if half >= 1:
                        item(zs, ys, half, 0).start()

                each(k, way, pass_on)

    for k in range(depth):
        for way in (1, 2) if k else (1,):
            def last(zs):
                for half in range(1, 5):
                    arrived(item(zs, 1 - y, half, 0))
                    sent(item(zs, y, half, 0))

            each(k, way, last)
    item(z, y, 0, 0).wait_send()
    for k in range(depth):
        for ys, half in kinds:
            for way in (1, 2):
                def drain(zs, ys=ys, half=half, way=way):
                    along(zs, ys, half, way, sent)

                each(k, way, drain)


def tail(grad, row_part, col_part, row_stat, col_stat, master):
    rows_n, cols_n = lax.axis_size("row"), lax.axis_size("col")
    height, width = grad.shape
    f32 = jnp.float32

    def eight(x):
        return jnp.broadcast_to(x, (8, x.shape[1]))

    vmem = pl.BlockSpec(memory_space=pltpu.VMEM)
    dma = pltpu.SemaphoreType.DMA
    items = rows_n * 5
    return pl.pallas_call(
        functools.partial(tail_kernel, rows_n, cols_n),
        out_shape=(
            jax.ShapeDtypeStruct((rows_n * height, width), jnp.bfloat16),
            jax.ShapeDtypeStruct((height, width), f32),
            jax.ShapeDtypeStruct((height, width), f32),
            jax.ShapeDtypeStruct((1, height), f32),
            jax.ShapeDtypeStruct((1, width), f32),
        ),
        in_specs=[vmem] * 6,
        out_specs=(vmem,) * 5,
        scratch_shapes=[
            pltpu.VMEM((cols_n, 8, height), f32),
            pltpu.VMEM((rows_n, 8, width), f32),
            pltpu.VMEM((height, 128), f32),
            pltpu.VMEM((16, 128), f32),
            pltpu.VMEM((rows_n, 16, 128), f32),
            pltpu.VMEM((8, 128), f32),
            pltpu.VMEM((cols_n, 8, 128), f32),
            dma((cols_n,)), dma((cols_n,)),
            dma((rows_n,)), dma((rows_n,)),
            dma((rows_n,)), dma((rows_n,)),
            dma((cols_n,)), dma((cols_n,)),
            dma((items * 3,)), dma((items,)),
        ],
        compiler_params=pltpu.CompilerParams(
            collective_id=0, has_side_effects=True, vmem_limit_bytes=40 * 1024 * 1024
        ),
    )(grad, eight(row_part), eight(col_part), eight(row_stat), eight(col_stat), master)


def shards(acts, out_grads, row_stat, col_stat, master):
    tok_here, mats, width_c = out_grads.shape
    flat_out = out_grads.reshape(tok_here, mats * width_c)
    rows_here = master.shape[0]
    if (lax.axis_size("row"), lax.axis_size("col"), mats) == (8, 4, 1):
        grad = gradient_rows(acts, flat_out)
        squares = grad * grad + 1e-30
        fresh, master_out, update_out, row_out, col_out = tail(
            grad,
            jnp.sum(squares, axis=1)[None],
            jnp.sum(squares, axis=0)[None],
            row_stat,
            col_stat,
            master.reshape(rows_here, width_c),
        )
        return (
            fresh.reshape(-1, mats, width_c),
            master_out.reshape(master.shape),
            update_out.reshape(master.shape),
            row_out,
            col_out,
        )
    else:
        acts_full = lax.all_gather(acts, "col", axis=1, tiled=True)
        grad = lax.psum_scatter(
            contract_tokens(acts_full, flat_out), "row", scatter_dimension=0, tiled=True
        )
    grad = grad.reshape(rows_here, mats, width_c)
    squares = grad * grad + 1e-30
    row_part = jnp.sum(squares, axis=2).T
    col_part = jnp.sum(squares, axis=0)
    row_sum = lax.psum(row_part, "col")
    row_out = 0.75 * row_stat + 0.25 * row_sum / D
    col_sum, row_total = lax.psum((col_part, jnp.sum(row_out, axis=1)), "row")
    col_out = 0.75 * col_stat + 0.25 * col_sum / D
    row_mean = row_total / D
    raw = grad * lax.rsqrt(row_out.T[:, :, None] * col_out[None, :, :] / row_mean[None, :, None])
    total_sq = lax.psum(jnp.sum(raw * raw, axis=(0, 2)), ("row", "col"))
    rms = jnp.sqrt(total_sq / (D * D))
    update_out = raw / jnp.maximum(1.0, rms)[None, :, None]
    master_out = master - 0.01 * update_out
    fresh = lax.all_gather(master_out.astype(jnp.bfloat16), "row", axis=0, tiled=True)
    return (fresh, master_out, update_out, row_out, col_out)


def solution(mesh):
    in_specs = (
        P("row", "col"),
        P("row", None, "col"),
        P(None, "row"),
        P(None, "col"),
        P("row", None, "col"),
    )
    out_specs = (
        P(None, None, "col"),
        P("row", None, "col"),
        P("row", None, "col"),
        P(None, "row"),
        P(None, "col"),
    )
    return jax.shard_map(shards, mesh=mesh, in_specs=in_specs, out_specs=out_specs, check_vma=False)
```
